512 devices in a mesh: dp: 4 (over x), expert: 8 (over z_lo, core), etp: 16 (over z_hi, y).
Axes of the slice: x: 4, y: 4, z: 16 (z_hi: 4, z_lo: 4; z = z_hi * 4 + z_lo), core: 2. Of those that a mesh axis runs over, the one named last changes fastest.
Arguments:
- tokens: bfloat16 [2048, 3072], P(('dp', 'expert', 'etp')), may hold values from -6 to 6
- expert_ids: int32 [2048, 2], P(('dp', 'expert', 'etp')), may hold values from 0 to 7, all different within a row; in each aligned block of 4 rows (0 to 3, 4 to 7, ...) at most 2 rows name the same one
- gate_probs: float32 [2048, 2], P(('dp', 'expert', 'etp')), may hold values from 0.1 to 0.9
- gate_weight: bfloat16 [8, 3072, 8192], P('expert', 'dp', 'etp'), may hold values from -0.109375 to 0.109375
- up_weight: bfloat16 [8, 3072, 8192], P('expert', 'dp', 'etp'), may hold values from -0.109375 to 0.109375
- down_weight: bfloat16 [8, 8192, 3072], P('expert', 'etp', 'dp'), may hold values from -0.0625 to 0.0625
- cotangent: bfloat16 [2048, 3072], P(('dp', 'expert', 'etp')), may hold values from -6 to 6
Outputs:
- layer_out: bfloat16 [2048, 3072], P(('dp', 'expert', 'etp'))
- token_grads: bfloat16 [2048, 3072], P(('dp', 'expert', 'etp'))
- down_grads: bfloat16 [8, 8192, 3072], P('expert', 'etp', 'dp')
The draws below stay inside these ranges and needn't reach their ends.
Inputs may be any that keep to these rules, and one draw needn't show every extreme that they name: `expert_ids`: each row names 2 different experts; among the 4 rows of one device no expert is named by more than 2 rows, a bound that some block reaches.
All inputs are finite; a program needn't handle non-finite values.
Results may differ from the reference program's by a relative error of at most 0.022.
Values may be sent and summed in bfloat16 or wider, within the bound.
No kernel may reach another device: no remote copies, remote signals or barrier semaphores. Data moves between devices by JAX's collectives and lax.ppermute only.
A program may use at most 64 MiB of HBM per device.

```python
import math
import jax
import jax.numpy as jnp
import numpy as np
from jax import lax

D = 3072
FF = 8192
TOP = 2
TOK_DEV = 4
EXPERTS = 8
CAP = 2
TOKENS = 2048
N_DP = 4
N_ETP = 16


def block_levels(own_key, shape, shards, least, high):
    factor_of, own = 1.0, jax.random.fold_in(own_key, 6)
    for position, shards_of in shards:
        heights = jnp.exp(jax.random.uniform(jax.random.fold_in(own, position), (shards_of,), jnp.float32, least / len(shards), high / len(shards)))
        factor_of = factor_of * jnp.repeat(heights, shape[position] // shards_of).reshape([-1 if axis == position else 1 for axis in range(len(shape))])
    return factor_of


def assign_block(stream_key, own, number, rows, amount, top, reach, skew):
    ranking = jax.random.permutation(stream_key, amount)
    heavy_load, ordinary = shares(amount, rows * top, reach, skew, True), shares(amount, rows * top, reach, skew, False)
    places = jnp.arange(amount)

    def named(tallies, rotation):
        used = int((tallies > 0).sum())
        fixed = max(1, used // 4)
        shifted = fixed + (places - fixed + rotation * (used - fixed)) % max(1, amount - fixed)
        return jnp.zeros((amount,), jnp.int32).at[ranking[jnp.where(places < fixed, places, shifted)]].set(jnp.asarray(tallies, jnp.int32))

    tallies = jnp.where(number % 4 == 0, named(heavy_load, number // 4), named(ordinary, number - number // 4 - 1))
    mixed = jax.random.permutation(jax.random.fold_in(own, 3), amount)
    source_of, receiver = mixed[0:amount // 2 * 2:2], mixed[1:amount // 2 * 2:2]
    margin = jnp.minimum(tallies[source_of] - 1, reach - tallies[receiver]) // 2
    margin = jnp.where((source_of == ranking[0]) | (receiver == ranking[0]) | (tallies[receiver] == 0), 0, jnp.maximum(margin, 0))
    shifted = jax.random.randint(jax.random.fold_in(own, 4), (amount // 2,), 0, 1 << 20) % (margin + 1)
    tallies = tallies.at[source_of].add(-shifted).at[receiver].add(shifted)
    labels = jnp.searchsorted(jnp.cumsum(tallies), jnp.arange(rows * top), side="right").astype(jnp.int32)
    listing = labels.reshape(top, rows).T
    listing = listing[jax.random.permutation(jax.random.fold_in(own, 1), rows)]
    rotation = jax.random.randint(jax.random.fold_in(own, 2), (rows, 1), 0, top)
    return jnp.take_along_axis(listing, (jnp.arange(top)[None, :] + rotation) % top, axis=1)


def shares(count, total, limit, lean, full):
    weights = [(1 << 20) // math.isqrt(standing ** lean) + 1 for standing in range(1, count + 1)]
    largest = limit if full else min(limit, max(-(-total // count), total * weights[0] // sum(weights)))
    least = 1 if total - largest >= count - 1 else 0
    counts, surplus = [largest] + [least] * (count - 1), total - largest - least * (count - 1)
    while surplus > 0:
        free = [i for i in range(1, count) if counts[i] < largest] or [i for i in range(1, count) if counts[i] < limit]
        whole, remaining = sum([weights[i] for i in free]), surplus
        for i in free:
            addition = min(limit - counts[i], max(1, remaining * weights[i] // whole), surplus)
            counts[i] = counts[i] + addition
            surplus = surplus - addition
    return np.array(counts)


def noise(stream_key, dims, scale, limit, split=(), kind=jnp.bfloat16):
    result = scale * jax.random.normal(stream_key, dims, jnp.float32)
    if split:
        result = result * block_levels(stream_key, dims, split, -0.22, 0.18)
    return jnp.clip(result, -limit, limit).astype(kind)


def setup_inputs(seed: int = 0) -> dict:
    key_list = jax.random.split(jax.random.key(seed), 8)
    tokens = noise(key_list[0], (TOKENS, D), 1.0, 6.0, ((0, 512),))
    expert_ids_keys = jax.random.split(jax.random.fold_in(key_list[1], 1), TOKENS // TOK_DEV)
    expert_ids_turns = jax.random.permutation(jax.random.fold_in(key_list[1], 3), TOKENS // TOK_DEV)
    expert_ids = jax.vmap(lambda own, number: assign_block(jax.random.fold_in(key_list[1], 2), own, number, TOK_DEV, EXPERTS, TOP, CAP, 2))(expert_ids_keys, expert_ids_turns).reshape((TOKENS, TOP))
    gate_probs = jnp.clip(0.1 + 0.79999997 * jax.random.uniform(key_list[2], (TOKENS, TOP), jnp.float32) ** block_levels(key_list[2], (TOKENS, TOP), ((0, 512),), -0.2, 0.2), 0.1, 0.9)
    gate_weight = noise(key_list[3], (EXPERTS, D, FF), D ** -0.5, 0.109375, ((0, 8), (1, 4), (2, 16)))
    up_weight = noise(key_list[4], (EXPERTS, D, FF), D ** -0.5, 0.109375, ((0, 8), (1, 4), (2, 16)))
    down_weight = noise(key_list[5], (EXPERTS, FF, D), FF ** -0.5, 0.0625, ((0, 8), (1, 16), (2, 4)))
    cotangent = noise(key_list[6], (TOKENS, D), 1.0, 6.0, ((0, 512),))
    return dict(tokens=tokens, expert_ids=expert_ids, gate_probs=gate_probs, gate_weight=gate_weight, up_weight=up_weight, down_weight=down_weight, cotangent=cotangent)


def reference(tokens, expert_ids, gate_probs, gate_weight, up_weight, down_weight, cotangent):
    slot_count = TOKENS * TOP
    most_rows = (TOKENS // TOK_DEV) * CAP
    ff_block = FF // N_ETP
    d_block = D // N_DP
    flat_ids = expert_ids.reshape(slot_count)
    flat_probs = gate_probs.reshape(slot_count)
    owner_index = jnp.arange(slot_count, dtype=jnp.int32) // TOP
    scaled = (flat_probs[:, None] * cotangent[owner_index].astype(jnp.float32)).astype(jnp.bfloat16)
    contract_last = (((1,), (1,)), ((), ()))

    def one_expert(expert):
        picked = jnp.nonzero(flat_ids == expert, size=most_rows, fill_value=slot_count)[0].astype(jnp.int32)
        is_valid = picked < slot_count
        safe_index = jnp.where(is_valid, picked, 0).astype(jnp.int32)
        token_rows = jnp.where(is_valid[:, None], tokens[safe_index // TOP], jnp.zeros((), jnp.bfloat16))
        cot_rows = jnp.where(is_valid[:, None], scaled[safe_index], jnp.zeros((), jnp.bfloat16))
        gate_mat = gate_weight[expert]
        up_mat = up_weight[expert]
        down_mat = down_weight[expert]
        gate_pre = jnp.dot(token_rows, gate_mat, preferred_element_type=jnp.float32)
        up_pre = jnp.dot(token_rows, up_mat, preferred_element_type=jnp.float32)
        sigmoid_gate = jax.nn.sigmoid(gate_pre)
        activated = gate_pre * sigmoid_gate
        slope_gate = sigmoid_gate * (1.0 + gate_pre * (1.0 - sigmoid_gate))
        hidden = (activated * up_pre).astype(jnp.bfloat16)
        out_rows = jnp.zeros((most_rows, D), jnp.float32)
        for block in range(N_ETP):
            lower = block * ff_block
            partial_sum = jnp.dot(hidden[:, lower:lower + ff_block], down_mat[lower:lower + ff_block], preferred_element_type=jnp.float32)
            out_rows = out_rows + lax.optimization_barrier(partial_sum.astype(jnp.bfloat16)).astype(jnp.float32)
        out_rows = out_rows.astype(jnp.bfloat16)
        grad_hidden = jnp.zeros((most_rows, FF), jnp.float32)
        for block in range(N_DP):
            lower = block * d_block
            partial_sum = lax.dot_general(cot_rows[:, lower:lower + d_block], down_mat[:, lower:lower + d_block], contract_last, preferred_element_type=jnp.float32)
            grad_hidden = grad_hidden + lax.optimization_barrier(partial_sum.astype(jnp.bfloat16)).astype(jnp.float32)
        grad_up = (grad_hidden * activated).astype(jnp.bfloat16)
        grad_gate = (grad_hidden * up_pre * slope_gate).astype(jnp.bfloat16)
        grad_rows = jnp.zeros((most_rows, D), jnp.float32)
        for block in range(N_ETP):
            lower = block * ff_block
            partial_sum = lax.dot_general(grad_gate[:, lower:lower + ff_block], gate_mat[:, lower:lower + ff_block], contract_last, preferred_element_type=jnp.float32)
            partial_sum = partial_sum + lax.dot_general(grad_up[:, lower:lower + ff_block], up_mat[:, lower:lower + ff_block], contract_last, preferred_element_type=jnp.float32)
            grad_rows = grad_rows + lax.optimization_barrier(partial_sum.astype(jnp.bfloat16)).astype(jnp.float32)
        grad_rows = grad_rows.astype(jnp.bfloat16)
        grad_down = jnp.dot(hidden.T, cot_rows, preferred_element_type=jnp.float32).astype(jnp.bfloat16)
        return picked, out_rows, grad_rows, grad_down

    picked, out_rows, grad_rows, down_grads = lax.map(one_expert, jnp.arange(EXPERTS, dtype=jnp.int32))
    flat_picked = picked.reshape(-1)
    slot_out = jnp.zeros((slot_count, D), jnp.bfloat16).at[flat_picked].set(out_rows.reshape(-1, D), mode="drop")
    slot_grad = jnp.zeros((slot_count, D), jnp.bfloat16).at[flat_picked].set(grad_rows.reshape(-1, D), mode="drop")
    layer_out = (flat_probs[:, None] * slot_out.astype(jnp.float32)).reshape(TOKENS, TOP, D).sum(axis=1).astype(jnp.bfloat16)
    token_grads = slot_grad.astype(jnp.float32).reshape(TOKENS, TOP, D).sum(axis=1).astype(jnp.bfloat16)
    return layer_out, token_grads, down_grads
```

```python
import jax
import jax.numpy as jnp
from jax import lax
from jax.sharding import Mesh
from jax.sharding import PartitionSpec as P

CAP = 2
META = 128
F32 = jnp.float32
BF16 = jnp.bfloat16
LAST = (((1,), (1,)), ((), ()))
FIRST = (((0,), (0,)), ((), ()))


def dot(a, b, dims=(((1,), (0,)), ((), ()))):
    return lax.dot_general(a, b, dims, preferred_element_type=F32)


def meta_columns(expert_ids, gate_probs):
    rows = expert_ids.shape[0]
    same = expert_ids[:, :, None, None] == expert_ids[None, None, :, :]
    earlier = jnp.arange(rows)[None, None, :, None] < jnp.arange(rows)[:, None, None, None]
    place = jnp.sum((same & earlier).astype(jnp.int32), axis=(2, 3))
    code = (expert_ids * CAP + place).astype(F32)
    high = lax.reduce_precision(gate_probs, 8, 7)
    rest = gate_probs - high
    middle = lax.reduce_precision(rest, 8, 7)
    low = rest - middle
    columns = jnp.concatenate([code, high, middle, low], axis=1).astype(BF16)
    return jnp.pad(columns, ((0, 0), (0, META - columns.shape[1])))


def slot_table(code, expert, block):
    count = code.shape[0]
    slots = count // block * CAP
    token = lax.broadcasted_iota(jnp.int32, (count, slots), 0)
    slot = lax.broadcasted_iota(jnp.int32, (count, slots), 1)
    wanted = expert * CAP + slot % CAP
    hit = (code[:, 0:1] == wanted) | (code[:, 1:2] == wanted)
    return (hit & (token // block == slot // CAP)).astype(BF16)


def gather_by_exchange(x, axes, size):
    spread = jnp.broadcast_to(x[None], (size,) + x.shape)
    return lax.all_to_all(spread, axes, split_axis=0, concat_axis=0, tiled=True).reshape(
        (size * x.shape[0],) + x.shape[1:]
    )


def scatter_sum_by_exchange(x, axes, size):
    parts = x.reshape((size, x.shape[0] // size) + x.shape[1:])
    parts = lax.all_to_all(parts, axes, split_axis=0, concat_axis=0, tiled=True)
    return jnp.sum(parts.astype(F32), axis=0).astype(BF16)


def on_device(tokens, expert_ids, gate_probs, gate_weight, up_weight, down_weight, cotangent):
    block, width = tokens.shape
    quarter = down_weight.shape[2]
    quarters = width // quarter
    y_size = lax.axis_size("y")
    z_size = lax.axis_size("zh") * lax.axis_size("zl")
    core = lax.axis_index("c")
    expert = lax.axis_index("zl") * 2 + core
    other = lax.axis_index("zl") * 2 + 1 - core

    full_gate = lax.all_gather(gate_weight[0], "x", axis=0, tiled=True)
    full_up = lax.all_gather(up_weight[0], "x", axis=0, tiled=True)
    full_down = lax.all_gather(down_weight[0], "x", axis=0)

    packed = jnp.concatenate([tokens, cotangent, meta_columns(expert_ids, gate_probs)], axis=1)
    along_z = gather_by_exchange(packed, ("zh", "zl"), z_size)
    plane = gather_by_exchange(along_z, "y", y_size)

    code = plane[:, 2 * width : 2 * width + 2].astype(jnp.int32)
    table_own = slot_table(code, expert, block)
    table_other = slot_table(code, other, block)
    half = table_own.shape[1]
    rows_own = dot(table_own, plane, FIRST).astype(BF16)
    rows_other = dot(table_other, plane, FIRST).astype(BF16)
    rows_arrived = lax.ppermute(rows_other, "c", [(0, 1), (1, 0)])
    rows = jnp.concatenate([rows_own, rows_arrived], axis=0)

    about = rows[:, 2 * width :].astype(F32)
    slot = lax.broadcasted_iota(jnp.int32, (2 * half, 1), 0)
    first = about[:, 0:1].astype(jnp.int32) == expert * CAP + slot % CAP
    prob0 = about[:, 2:3] + about[:, 4:5] + about[:, 6:7]
    prob1 = about[:, 3:4] + about[:, 5:6] + about[:, 7:8]
    prob = jnp.where(first, prob0, prob1)
    token_rows = rows[:, :width]
    cot_rows = (prob * rows[:, width : 2 * width].astype(F32)).astype(BF16)

    gate_pre = dot(token_rows, full_gate)
    up_pre = dot(token_rows, full_up)
    sigmoid_gate = jax.nn.sigmoid(gate_pre)
    activated = gate_pre * sigmoid_gate
    slope_gate = sigmoid_gate * (1.0 + gate_pre * (1.0 - sigmoid_gate))
    hidden = (activated * up_pre).astype(BF16)

    partial_down = jnp.stack(
        [
            dot(hidden, cot_rows[:, q * quarter : (q + 1) * quarter], FIRST).astype(BF16)
            for q in range(quarters)
        ]
    )
    down_grads = lax.psum_scatter(partial_down, "x", scatter_dimension=0)[None]

    grad_hidden = sum(
        dot(cot_rows[:, q * quarter : (q + 1) * quarter], full_down[q], LAST)
        for q in range(quarters)
    )
    grad_up = (grad_hidden * activated).astype(BF16)
    grad_gate = (grad_hidden * up_pre * slope_gate).astype(BF16)
    out_part = [(prob * dot(hidden, full_down[q])).astype(BF16) for q in range(quarters)]
    grad_part = (dot(grad_gate, full_gate, LAST) + dot(grad_up, full_up, LAST)).astype(BF16)
    both = jnp.concatenate(out_part + [grad_part], axis=1)

    returned = lax.ppermute(both[half:], "c", [(0, 1), (1, 0)])
    by_token = (dot(table_own, both[:half]) + dot(table_other, returned)).astype(BF16)
    along_z = scatter_sum_by_exchange(by_token, "y", y_size)
    own = scatter_sum_by_exchange(along_z, ("zh", "zl"), z_size)
    return own[:, :width], own[:, width:], down_grads


def finer(mesh):
    dp, experts, etp = (mesh.shape[name] for name in ("dp", "expert", "etp"))
    high = 4 if etp % 4 == 0 else 2
    shape = (dp, experts // 2, 2, high, etp // high)
    return Mesh(mesh.devices.reshape(shape), ("x", "zl", "c", "zh", "y"))


def solution(mesh):
    rows = P(("x", "zl", "c", "zh", "y"), None)
    columns = P(("zl", "c"), "x", ("zh", "y"))
    depth = P(("zl", "c"), ("zh", "y"), "x")
    return jax.shard_map(
        on_device,
        mesh=finer(mesh),
        in_specs=(rows, rows, rows, columns, columns, depth, rows),
        out_specs=(rows, rows, depth),
        check_vma=False,
    )
```

```python
import jax
import jax.numpy as jnp
from jax import lax
from jax.experimental.layout import Layout, with_layout_constraint
from jax.sharding import Mesh
from jax.sharding import PartitionSpec as P

CAP = 2
META = 128
F32 = jnp.float32
BF16 = jnp.bfloat16
LAST = (((1,), (1,)), ((), ()))
FIRST = (((0,), (0,)), ((), ()))


def dot(a, b, dims=(((1,), (0,)), ((), ()))):
    return lax.dot_general(a, b, dims, preferred_element_type=F32)


def meta_columns(expert_ids, gate_probs):
    rows = expert_ids.shape[0]
    same = expert_ids[:, :, None, None] == expert_ids[None, None, :, :]
    earlier = jnp.arange(rows)[None, None, :, None] < jnp.arange(rows)[:, None, None, None]
    place = jnp.sum((same & earlier).astype(jnp.int32), axis=(2, 3))
    code = (expert_ids * CAP + place).astype(F32)
    high = lax.reduce_precision(gate_probs, 8, 7)
    rest = gate_probs - high
    middle = lax.reduce_precision(rest, 8, 7)
    low = rest - middle
    columns = jnp.concatenate([code, high, middle, low], axis=1).astype(BF16)
    return jnp.pad(columns, ((0, 0), (0, META - columns.shape[1])))


def slot_table(code, expert, block):
    count = code.shape[0]
    slots = count // block * CAP
    token = lax.broadcasted_iota(jnp.int32, (count, slots), 0)
    slot = lax.broadcasted_iota(jnp.int32, (count, slots), 1)
    wanted = expert * CAP + slot % CAP
    hit = (code[:, 0:1] == wanted) | (code[:, 1:2] == wanted)
    return (hit & (token // block == slot // CAP)).astype(BF16)


def gather_by_exchange(x, axes, size):
    spread = jnp.broadcast_to(x[None], (size,) + x.shape)
    return lax.all_to_all(spread, axes, split_axis=0, concat_axis=0, tiled=True).reshape(
        (size * x.shape[0],) + x.shape[1:]
    )


def scatter_sum_by_exchange(x, axes, size):
    parts = x.reshape((size, x.shape[0] // size) + x.shape[1:])
    parts = lax.all_to_all(parts, axes, split_axis=0, concat_axis=0, tiled=True)
    return jnp.sum(parts.astype(F32), axis=0).astype(BF16)


def send_by_shifts(x, axis, size):
    rows = x.shape[0] // size
    here = lax.axis_index(axis)

    def block(shift):
        return lax.dynamic_slice_in_dim(x, lax.rem(here + shift, size) * rows, rows, axis=0)

    parts = [block(0)]
    for shift in range(1, size):
        pairs = [(i, (i + shift) % size) for i in range(size)]
        parts.append(lax.ppermute(block(shift), axis, pairs))
    return parts


def add_up(parts):
    return sum(part.astype(F32) for part in parts).astype(BF16)


def on_device(tokens, expert_ids, gate_probs, gate_weight, up_weight, down_weight, cotangent):
    block, width = tokens.shape
    quarter = down_weight.shape[2]
    quarters = width // quarter
    y_size = lax.axis_size("y")
    z_size = lax.axis_size("zh") * lax.axis_size("zl")
    core = lax.axis_index("c")
    expert = lax.axis_index("zl") * 2 + core
    other = lax.axis_index("zl") * 2 + 1 - core

    mine = jnp.concatenate([gate_weight[0], up_weight[0], down_weight[0].T], axis=1)
    mine = with_layout_constraint(mine, Layout(major_to_minor=(0, 1)))
    weights = lax.all_gather(mine, "x", axis=0, tiled=True)
    ff = gate_weight.shape[2]
    full_both, full_down = weights[:, : 2 * ff], weights[:, 2 * ff :]

    packed = jnp.concatenate([tokens, cotangent, meta_columns(expert_ids, gate_probs)], axis=1)
    by_z = gather_by_exchange(packed, ("zh", "zl"), z_size)
    plane = gather_by_exchange(by_z, "y", y_size)

    code = plane[:, 2 * width : 2 * width + 2].astype(jnp.int32)
    table_own = slot_table(code, expert, block)
    table_other = slot_table(code, other, block)
    half = table_own.shape[1]
    rows_own = dot(table_own, plane, FIRST).astype(BF16)
    rows_other = dot(table_other, plane, FIRST).astype(BF16)
    rows_arrived = lax.ppermute(rows_other, "c", [(0, 1), (1, 0)])
    rows = jnp.concatenate([rows_own, rows_arrived], axis=0)

    about = rows[:, 2 * width :].astype(F32)
    slot = lax.broadcasted_iota(jnp.int32, (2 * half, 1), 0)
    first = about[:, 0:1].astype(jnp.int32) == expert * CAP + slot % CAP
    prob0 = about[:, 2:3] + about[:, 4:5] + about[:, 6:7]
    prob1 = about[:, 3:4] + about[:, 5:6] + about[:, 7:8]
    prob = jnp.where(first, prob0, prob1)
    token_rows = rows[:, :width]
    cot_rows = (prob * rows[:, width : 2 * width].astype(F32)).astype(BF16)

    def leave(part):
        returned = lax.ppermute(part[half:], "c", [(0, 1), (1, 0)])
        return (dot(table_own, part[:half]) + dot(table_other, returned)).astype(BF16)

    def along_z(parts):
        return scatter_sum_by_exchange(add_up(parts), ("zh", "zl"), z_size)

    gate_up = dot(token_rows, full_both)
    gate_pre, up_pre = gate_up[:, :ff], gate_up[:, ff:]
    sigmoid_gate = jax.nn.sigmoid(gate_pre)
    activated = gate_pre * sigmoid_gate
    slope_gate = sigmoid_gate * (1.0 + gate_pre * (1.0 - sigmoid_gate))
    hidden = (activated * up_pre).astype(BF16)
    out_part = (prob * dot(hidden, full_down, LAST)).astype(BF16)
    out_tokens = leave(out_part)
    out_parts = send_by_shifts(out_tokens, "y", y_size)

    late_hidden, late_cot, _ = lax.optimization_barrier((hidden, cot_rows, out_tokens))
    grad_hidden = dot(late_cot, full_down)
    grad_up = (grad_hidden * activated).astype(BF16)
    grad_gate = (grad_hidden * up_pre * slope_gate).astype(BF16)
    grad_both = jnp.concatenate([grad_gate, grad_up], axis=1)
    grad_tokens = leave(dot(grad_both, full_both, LAST).astype(BF16))

    grad_parts = send_by_shifts(grad_tokens, "y", y_size)

    partial_down = jnp.stack(
        [
            dot(late_hidden, late_cot[:, q * quarter : (q + 1) * quarter], FIRST).astype(BF16)
            for q in range(quarters)
        ]
    )
    down_grads = lax.psum_scatter(partial_down, "x", scatter_dimension=0)[None]
    layer_out = along_z(out_parts)
    grad_parts, layer_out = lax.optimization_barrier((grad_parts, layer_out))
    return layer_out, along_z(grad_parts), down_grads


def finer(mesh):
    dp, experts, etp = (mesh.shape[name] for name in ("dp", "expert", "etp"))
    high = 4 if etp % 4 == 0 else 2
    shape = (dp, experts // 2, 2, high, etp // high)
    return Mesh(mesh.devices.reshape(shape), ("x", "zl", "c", "zh", "y"))


def solution(mesh):
    rows = P(("x", "zl", "c", "zh", "y"), None)
    columns = P(("zl", "c"), "x", ("zh", "y"))
    depth = P(("zl", "c"), ("zh", "y"), "x")
    return jax.shard_map(
        on_device,
        mesh=finer(mesh),
        in_specs=(rows, rows, rows, columns, columns, depth, rows),
        out_specs=(rows, rows, depth),
        check_vma=False,
    )
```

```python
import jax
import jax.numpy as jnp
from jax import lax
from jax.experimental.layout import Layout, with_layout_constraint
from jax.sharding import Mesh
from jax.sharding import PartitionSpec as P

CAP = 2
META = 128
F32 = jnp.float32
BF16 = jnp.bfloat16
LAST = (((1,), (1,)), ((), ()))
FIRST = (((0,), (0,)), ((), ()))


def dot(a, b, dims=(((1,), (0,)), ((), ()))):
    return lax.dot_general(a, b, dims, preferred_element_type=F32)


def meta_columns(expert_ids, gate_probs):
    rows = expert_ids.shape[0]
    same = expert_ids[:, :, None, None] == expert_ids[None, None, :, :]
    earlier = jnp.arange(rows)[None, None, :, None] < jnp.arange(rows)[:, None, None, None]
    place = jnp.sum((same & earlier).astype(jnp.int32), axis=(2, 3))
    code = (expert_ids * CAP + place).astype(F32)
    high = lax.reduce_precision(gate_probs, 8, 7)
    rest = gate_probs - high
    middle = lax.reduce_precision(rest, 8, 7)
    low = rest - middle
    columns = jnp.concatenate([code, high, middle, low], axis=1).astype(BF16)
    return jnp.pad(columns, ((0, 0), (0, META - columns.shape[1])))


def slot_table(code, token, expert, block):
    slots = code.shape[0] // block * CAP
    slot = lax.broadcasted_iota(jnp.int32, (1, slots), 1)
    wanted = expert * CAP + slot % CAP
    hit = (code[:, 0:1] == wanted) | (code[:, 1:2] == wanted)
    return (hit & (token // block == slot // CAP)).astype(BF16)


def gather_by_exchange(x, axes, size):
    spread = jnp.broadcast_to(x[None], (size,) + x.shape)
    return lax.all_to_all(spread, axes, split_axis=0, concat_axis=0, tiled=True).reshape(
        (size * x.shape[0],) + x.shape[1:]
    )


def scatter_sum_by_exchange(x, axes, size):
    parts = x.reshape((size, x.shape[0] // size) + x.shape[1:])
    parts = lax.all_to_all(parts, axes, split_axis=0, concat_axis=0, tiled=True)
    return jnp.sum(parts.astype(F32), axis=0).astype(BF16)


def send_by_shifts(x, axis, size):
    rows = x.shape[0] // size
    here = lax.axis_index(axis)

    def block(shift):
        return lax.dynamic_slice_in_dim(x, lax.rem(here + shift, size) * rows, rows, axis=0)

    parts = [block(0)]
    for shift in range(1, size):
        pairs = [(i, (i + shift) % size) for i in range(size)]
        parts.append(lax.ppermute(block(shift), axis, pairs))
    return parts


def add_up(parts):
    return sum(part.astype(F32) for part in parts).astype(BF16)


def pass_on(x, axis, shift):
    size = lax.axis_size(axis)
    return lax.ppermute(x, axis, [(i, (i + shift) % size) for i in range(size)])


def roll_columns(x, start):
    return lax.dynamic_slice_in_dim(jnp.concatenate([x, x], axis=1), start, x.shape[1], axis=1)


def on_device(tokens, expert_ids, gate_probs, gate_weight, up_weight, down_weight, cotangent):
    block, width = tokens.shape
    ff = gate_weight.shape[2]
    quarter = down_weight.shape[2]
    quarters = width // quarter
    y_size, low_size, high_size = (lax.axis_size(name) for name in ("y", "zl", "zh"))
    group = lax.axis_index("x")
    core = lax.axis_index("c")
    expert = lax.axis_index("zl") * 2 + core
    other = lax.axis_index("zl") * 2 + 1 - core

    def columns(x, q):
        return x[:, q * quarter : (q + 1) * quarter]

    mine = jnp.concatenate([gate_weight[0], up_weight[0]], axis=1)
    mine = with_layout_constraint(mine, Layout(major_to_minor=(0, 1)))
    own_down, mine = lax.optimization_barrier((down_weight[0], mine))
    full_both = lax.all_gather(mine, "x", axis=0, tiled=True)
    from_next = pass_on(own_down, "x", -1)
    from_last = pass_on(own_down, "x", 1)

    turned = roll_columns(cotangent, group * quarter)
    packed = jnp.concatenate([tokens, turned, meta_columns(expert_ids, gate_probs)], axis=1)
    by_z = lax.all_gather(packed[None], ("zh", "zl"), axis=0, tiled=True)
    by_z, from_next, from_last = lax.optimization_barrier((by_z, from_next, from_last))
    plane = gather_by_exchange(by_z.reshape(-1, packed.shape[1]), "y", y_size)
    if quarters == 4:
        across = pass_on(from_next[: ff // 2], "x", -1), pass_on(from_last[ff // 2 :], "x", 1)
        plane, across = lax.optimization_barrier((plane, across))
        downs = [own_down, from_next, jnp.concatenate(across, axis=0), from_last]
    else:
        downs = [own_down, from_next]

    count = plane.shape[0]
    code = plane[:, 2 * width : 2 * width + 2].astype(jnp.int32)
    place = lax.broadcasted_iota(jnp.int32, (count, 1), 0)
    table_own = slot_table(code, place, expert, block)
    table_other = slot_table(code, place, other, block)
    half = table_own.shape[1]
    rows_own = dot(table_own, plane, FIRST).astype(BF16)
    rows_other = dot(table_other, plane, FIRST).astype(BF16)
    rows_arrived = lax.ppermute(rows_other, "c", [(0, 1), (1, 0)])
    rows = jnp.concatenate([rows_own, rows_arrived], axis=0)

    def low_first(x):
        split = x.reshape(y_size, high_size, low_size, block, x.shape[1])
        return split.transpose(0, 2, 1, 3, 4).reshape(x.shape)

    code_back = low_first(code)
    place_back = low_first(place)
    back_own = slot_table(code_back, place_back, expert, block)
    back_other = slot_table(code_back, place_back, other, block)

    about = rows[:, 2 * width :].astype(F32)
    slot = lax.broadcasted_iota(jnp.int32, (2 * half, 1), 0)
    first = about[:, 0:1].astype(jnp.int32) == expert * CAP + slot % CAP
    prob0 = about[:, 2:3] + about[:, 4:5] + about[:, 6:7]
    prob1 = about[:, 3:4] + about[:, 5:6] + about[:, 7:8]
    prob = jnp.where(first, prob0, prob1)
    token_rows = rows[:, :width]
    cot_rows = (prob * rows[:, width : 2 * width].astype(F32)).astype(BF16)

    def leave(part):
        returned = lax.ppermute(part[half:], "c", [(0, 1), (1, 0)])
        return (dot(back_own, part[:half]) + dot(back_other, returned)).astype(BF16)

    gate_up = dot(token_rows, full_both)
    gate_pre, up_pre = gate_up[:, :ff], gate_up[:, ff:]
    sigmoid_gate = jax.nn.sigmoid(gate_pre)
    activated = gate_pre * sigmoid_gate
    slope_gate = sigmoid_gate * (1.0 + gate_pre * (1.0 - sigmoid_gate))
    hidden = (activated * up_pre).astype(BF16)
    out_part = jnp.concatenate([(prob * dot(hidden, down)).astype(BF16) for down in downs], axis=1)
    out_tokens = leave(out_part)
    out_parts = send_by_shifts(out_tokens, "y", y_size)

    late_hidden, _ = lax.optimization_barrier((hidden, out_part))
    late_cot, _ = lax.optimization_barrier((cot_rows, out_tokens))
    grad_hidden = sum(dot(columns(late_cot, s), downs[s], LAST) for s in range(quarters))
    grad_up = (grad_hidden * activated).astype(BF16)
    grad_gate = (grad_hidden * up_pre * slope_gate).astype(BF16)
    grad_both = jnp.concatenate([grad_gate, grad_up], axis=1)
    grad_tokens = leave(dot(grad_both, full_both, LAST).astype(BF16))
    grad_parts = send_by_shifts(grad_tokens, "y", y_size)

    partial_down = []
    for q in range(quarters):
        start = lax.rem(q - group + quarters, quarters) * quarter
        block_q = lax.dynamic_slice_in_dim(cot_rows, start, quarter, axis=1)
        partial_down.append(dot(late_hidden, block_q, FIRST).astype(BF16))
    down_grads = lax.psum_scatter(jnp.stack(partial_down), "x", scatter_dimension=0)[None]

    out_y, grad_tokens = lax.optimization_barrier((add_up(out_parts), grad_tokens))
    out_low = scatter_sum_by_exchange(out_y, "zl", low_size)
    grad_low = scatter_sum_by_exchange(add_up(grad_parts), "zl", low_size)
    low = jnp.concatenate([out_low, grad_low], axis=1)
    own = scatter_sum_by_exchange(low, "zh", high_size)
    turn_back = lax.rem(quarters - group, quarters) * quarter
    return roll_columns(own[:, :width], turn_back), own[:, width:], down_grads


def finer(mesh):
    dp, experts, etp = (mesh.shape[name] for name in ("dp", "expert", "etp"))
    high = 4 if etp % 4 == 0 else 2
    shape = (dp, experts // 2, 2, high, etp // high)
    return Mesh(mesh.devices.reshape(shape), ("x", "zl", "c", "zh", "y"))


def solution(mesh):
    rows = P(("x", "zl", "c", "zh", "y"), None)
    columns = P(("zl", "c"), "x", ("zh", "y"))
    depth = P(("zl", "c"), ("zh", "y"), "x")
    return jax.shard_map(
        on_device,
        mesh=finer(mesh),
        in_specs=(rows, rows, rows, columns, columns, depth, rows),
        out_specs=(rows, rows, depth),
        check_vma=False,
    )
```

```python
import jax
import jax.numpy as jnp
from jax import lax
from jax.experimental.layout import Layout, with_layout_constraint
from jax.sharding import Mesh
from jax.sharding import PartitionSpec as P

CAP = 2
META = 128
F32 = jnp.float32
BF16 = jnp.bfloat16
LAST = (((1,), (1,)), ((), ()))
FIRST = (((0,), (0,)), ((), ()))


def dot(a, b, dims=(((1,), (0,)), ((), ()))):
    return lax.dot_general(a, b, dims, preferred_element_type=F32)


def meta_columns(expert_ids, gate_probs):
    rows = expert_ids.shape[0]
    same = expert_ids[:, :, None, None] == expert_ids[None, None, :, :]
    earlier = jnp.arange(rows)[None, None, :, None] < jnp.arange(rows)[:, None, None, None]
    place = jnp.sum((same & earlier).astype(jnp.int32), axis=(2, 3))
    code = (expert_ids * CAP + place).astype(F32)
    high = lax.reduce_precision(gate_probs, 8, 7)
    rest = gate_probs - high
    middle = lax.reduce_precision(rest, 8, 7)
    low = rest - middle
    columns = jnp.concatenate([code, high, middle, low], axis=1).astype(BF16)
    return jnp.pad(columns, ((0, 0), (0, META - columns.shape[1])))


def slot_table(code, token, expert, block):
    slots = code.shape[0] // block * CAP
    slot = lax.broadcasted_iota(jnp.int32, (1, slots), 1)
    wanted = expert * CAP + slot % CAP
    hit = (code[:, 0:1] == wanted) | (code[:, 1:2] == wanted)
    return (hit & (token // block == slot // CAP)).astype(BF16)


def gather_by_exchange(x, axes, size):
    spread = jnp.broadcast_to(x[None], (size,) + x.shape)
    return lax.all_to_all(spread, axes, split_axis=0, concat_axis=0, tiled=True).reshape(
        (size * x.shape[0],) + x.shape[1:]
    )


def scatter_sum_by_exchange(x, axes, size):
    parts = x.reshape((size, x.shape[0] // size) + x.shape[1:])
    parts = lax.all_to_all(parts, axes, split_axis=0, concat_axis=0, tiled=True)
    return jnp.sum(parts.astype(F32), axis=0).astype(BF16)


def send_by_shifts(x, axis, size):
    rows = x.shape[0] // size
    here = lax.axis_index(axis)

    def block(shift):
        return lax.dynamic_slice_in_dim(x, lax.rem(here + shift, size) * rows, rows, axis=0)

    parts = [block(0)]
    for shift in range(1, size):
        pairs = [(i, (i + shift) % size) for i in range(size)]
        parts.append(lax.ppermute(block(shift), axis, pairs))
    return parts


def add_up(parts):
    return sum(part.astype(F32) for part in parts).astype(BF16)


def pass_on(x, axis, shift):
    size = lax.axis_size(axis)
    return lax.ppermute(x, axis, [(i, (i + shift) % size) for i in range(size)])


def roll_columns(x, start):
    return lax.dynamic_slice_in_dim(jnp.concatenate([x, x], axis=1), start, x.shape[1], axis=1)


def on_device(tokens, expert_ids, gate_probs, gate_weight, up_weight, down_weight, cotangent):
    block, width = tokens.shape
    ff = gate_weight.shape[2]
    quarter = down_weight.shape[2]
    quarters = width // quarter
    y_size, low_size, high_size = (lax.axis_size(name) for name in ("y", "zl", "zh"))
    group = lax.axis_index("x")
    core = lax.axis_index("c")
    expert = lax.axis_index("zl") * 2 + core
    other = lax.axis_index("zl") * 2 + 1 - core

    mine = jnp.concatenate([gate_weight[0], up_weight[0]], axis=1)
    mine = with_layout_constraint(mine, Layout(major_to_minor=(0, 1)))
    own_down, mine = lax.optimization_barrier((down_weight[0], mine))
    full_both = lax.all_gather(mine, "x", axis=0, tiled=True)
    from_next = pass_on(own_down, "x", -1)
    from_last = pass_on(own_down, "x", 1)

    turned = roll_columns(cotangent, group * quarter)
    packed = jnp.concatenate([tokens, turned, meta_columns(expert_ids, gate_probs)], axis=1)
    by_z = lax.all_gather(packed[None], ("zh", "zl"), axis=0, tiled=True)
    by_z, from_next, from_last = lax.optimization_barrier((by_z, from_next, from_last))
    plane = gather_by_exchange(by_z.reshape(-1, packed.shape[1]), "y", y_size)
    if quarters == 4:
        cut = quarter // 2
        across = pass_on(from_next[:, :cut], "x", -1), pass_on(from_last[:, cut:], "x", 1)
        plane, across = lax.optimization_barrier((plane, across))
        downs = [own_down, from_next, *across, from_last]
    else:
        downs = [own_down, from_next]

    count = plane.shape[0]
    code = plane[:, 2 * width : 2 * width + 2].astype(jnp.int32)
    place = lax.broadcasted_iota(jnp.int32, (count, 1), 0)
    table_own = slot_table(code, place, expert, block)
    table_other = slot_table(code, place, other, block)
    half = table_own.shape[1]
    rows_own = dot(table_own, plane, FIRST).astype(BF16)
    rows_other = dot(table_other, plane, FIRST).astype(BF16)
    rows_arrived = lax.ppermute(rows_other, "c", [(0, 1), (1, 0)])
    rows = jnp.concatenate([rows_own, rows_arrived], axis=0)

    def low_first(x):
        split = x.reshape(y_size, high_size, low_size, block, x.shape[1])
        return split.transpose(0, 2, 1, 3, 4).reshape(x.shape)

    code_back = low_first(code)
    place_back = low_first(place)
    back_own = slot_table(code_back, place_back, expert, block)
    back_other = slot_table(code_back, place_back, other, block)

    about = rows[:, 2 * width :].astype(F32)
    slot = lax.broadcasted_iota(jnp.int32, (2 * half, 1), 0)
    first = about[:, 0:1].astype(jnp.int32) == expert * CAP + slot % CAP
    prob0 = about[:, 2:3] + about[:, 4:5] + about[:, 6:7]
    prob1 = about[:, 3:4] + about[:, 5:6] + about[:, 7:8]
    prob = jnp.where(first, prob0, prob1)
    token_rows = rows[:, :width]
    cot_rows = (prob * rows[:, width : 2 * width].astype(F32)).astype(BF16)

    def leave(part):
        returned = lax.ppermute(part[half:], "c", [(0, 1), (1, 0)])
        return (dot(back_own, part[:half]) + dot(back_other, returned)).astype(BF16)

    gate_up = dot(token_rows, full_both)
    gate_pre, up_pre = gate_up[:, :ff], gate_up[:, ff:]
    sigmoid_gate = jax.nn.sigmoid(gate_pre)
    activated = gate_pre * sigmoid_gate
    slope_gate = sigmoid_gate * (1.0 + gate_pre * (1.0 - sigmoid_gate))
    hidden = (activated * up_pre).astype(BF16)
    out_part = jnp.concatenate([(prob * dot(hidden, down)).astype(BF16) for down in downs], axis=1)
    out_tokens = leave(out_part)
    out_y = scatter_sum_by_exchange(out_tokens, "y", y_size)

    late_cot, _ = lax.optimization_barrier((cot_rows, out_part))
    grad_hidden, column = 0.0, 0
    for down in downs:
        piece = late_cot[:, column : column + down.shape[1]]
        grad_hidden, column = grad_hidden + dot(piece, down, LAST), column + down.shape[1]
    grad_up = (grad_hidden * activated).astype(BF16)
    grad_gate = (grad_hidden * up_pre * slope_gate).astype(BF16)
    grad_both = jnp.concatenate([grad_gate, grad_up], axis=1)
    grad_both, late_hidden, _ = lax.optimization_barrier((grad_both, hidden, out_tokens))
    grad_tokens = leave(dot(grad_both, full_both, LAST).astype(BF16))
    partial_down = []
    for q in range(quarters):
        start = lax.rem(q - group + quarters, quarters) * quarter
        block_q = lax.dynamic_slice_in_dim(late_cot, start, quarter, axis=1)
        partial_down.append(dot(late_hidden, block_q, FIRST).astype(BF16))
    partial_down = jnp.stack(partial_down)
    out_y, grad_tokens, partial_down = lax.optimization_barrier((out_y, grad_tokens, partial_down))
    down_grads = lax.psum_scatter(partial_down, "x", scatter_dimension=0)[None]

    grad_y = scatter_sum_by_exchange(grad_tokens, "y", y_size)
    out_low = add_up(send_by_shifts(out_y, "zl", low_size))
    out_low, grad_y = lax.optimization_barrier((out_low, grad_y))
    grad_low = scatter_sum_by_exchange(grad_y, "zl", low_size)
    low = jnp.concatenate([out_low, grad_low], axis=1)
    own = scatter_sum_by_exchange(low, "zh", high_size)
    turn_back = lax.rem(quarters - group, quarters) * quarter
    return roll_columns(own[:, :width], turn_back), own[:, width:], down_grads


def finer(mesh):
    dp, experts, etp = (mesh.shape[name] for name in ("dp", "expert", "etp"))
    high = 4 if etp % 4 == 0 else 2
    shape = (dp, experts // 2, 2, high, etp // high)
    return Mesh(mesh.devices.reshape(shape), ("x", "zl", "c", "zh", "y"))


def solution(mesh):
    rows = P(("x", "zl", "c", "zh", "y"), None)
    columns = P(("zl", "c"), "x", ("zh", "y"))
    depth = P(("zl", "c"), ("zh", "y"), "x")
    return jax.shard_map(
        on_device,
        mesh=finer(mesh),
        in_specs=(rows, rows, rows, columns, columns, depth, rows),
        out_specs=(rows, rows, depth),
        check_vma=False,
    )
```

```python
import jax
import jax.numpy as jnp
from jax import lax
from jax.experimental import pallas as pl
from jax.experimental.layout import Layout, with_layout_constraint
from jax.experimental.pallas import tpu as pltpu
from jax.sharding import Mesh
from jax.sharding import PartitionSpec as P

CAP = 2
META = 128
F32 = jnp.float32
BF16 = jnp.bfloat16
LAST = (((1,), (1,)), ((), ()))
FIRST = (((0,), (0,)), ((), ()))


def dot(a, b, dims=(((1,), (0,)), ((), ()))):
    return lax.dot_general(a, b, dims, preferred_element_type=F32)


def meta_columns(expert_ids, gate_probs):
    rows = expert_ids.shape[0]
    same = expert_ids[:, :, None, None] == expert_ids[None, None, :, :]
    earlier = jnp.arange(rows)[None, None, :, None] < jnp.arange(rows)[:, None, None, None]
    place = jnp.sum((same & earlier).astype(jnp.int32), axis=(2, 3))
    code = (expert_ids * CAP + place).astype(F32)
    high = lax.reduce_precision(gate_probs, 8, 7)
    rest = gate_probs - high
    middle = lax.reduce_precision(rest, 8, 7)
    low = rest - middle
    columns = jnp.concatenate([code, high, middle, low], axis=1).astype(BF16)
    return jnp.pad(columns, ((0, 0), (0, META - columns.shape[1])))


def slot_table(code, token, expert, block):
    slots = code.shape[0] // block * CAP
    slot = lax.broadcasted_iota(jnp.int32, (1, slots), 1)
    wanted = expert * CAP + slot % CAP
    hit = (code[:, 0:1] == wanted) | (code[:, 1:2] == wanted)
    return (hit & (token // block == slot // CAP)).astype(BF16)


def gather_by_exchange(x, axes, size):
    spread = jnp.broadcast_to(x[None], (size,) + x.shape)
    return lax.all_to_all(spread, axes, split_axis=0, concat_axis=0, tiled=True).reshape(
        (size * x.shape[0],) + x.shape[1:]
    )


def scatter_sum_by_exchange(x, axes, size):
    parts = x.reshape((size, x.shape[0] // size) + x.shape[1:])
    parts = lax.all_to_all(parts, axes, split_axis=0, concat_axis=0, tiled=True)
    return jnp.sum(parts.astype(F32), axis=0).astype(BF16)


def send_by_shifts(x, axis, size):
    rows = x.shape[0] // size
    here = lax.axis_index(axis)

    def block(shift):
        return lax.dynamic_slice_in_dim(x, lax.rem(here + shift, size) * rows, rows, axis=0)

    parts = [block(0)]
    for shift in range(1, size):
        pairs = [(i, (i + shift) % size) for i in range(size)]
        parts.append(lax.ppermute(block(shift), axis, pairs))
    return parts


def add_up(parts):
    return sum(part.astype(F32) for part in parts).astype(BF16)


def pass_on(x, axis, shift):
    size = lax.axis_size(axis)
    return lax.ppermute(x, axis, [(i, (i + shift) % size) for i in range(size)])


def product_kernel(*refs):
    rows_ref, block_refs, total_ref = refs[0], refs[1:-1], refs[-1]
    column, total = 0, 0.0
    for block_ref in block_refs:
        size = block_ref.shape[1]
        piece = rows_ref[:, column : column + size]
        total, column = total + dot(piece, block_ref[...], LAST), column + size
    total_ref[...] = total


def product(rows, blocks):
    return pl.pallas_call(
        product_kernel,
        out_shape=jax.ShapeDtypeStruct((rows.shape[0], blocks[0].shape[0]), F32),
        in_specs=[pl.BlockSpec(memory_space=pltpu.VMEM)] * (1 + len(blocks)),
        out_specs=pl.BlockSpec(memory_space=pltpu.VMEM),
        compiler_params=pltpu.CompilerParams(vmem_limit_bytes=24 * 1024 * 1024),
        cost_estimate=pl.CostEstimate(flops=1000, bytes_accessed=1000, transcendentals=0),
    )(rows, *blocks)


def roll_columns(x, start):
    return lax.dynamic_slice_in_dim(jnp.concatenate([x, x], axis=1), start, x.shape[1], axis=1)


def on_device(tokens, expert_ids, gate_probs, gate_weight, up_weight, down_weight, cotangent):
    block, width = tokens.shape
    ff = gate_weight.shape[2]
    quarter = down_weight.shape[2]
    quarters = width // quarter
    y_size, low_size, high_size = (lax.axis_size(name) for name in ("y", "zl", "zh"))
    group = lax.axis_index("x")
    core = lax.axis_index("c")
    expert = lax.axis_index("zl") * 2 + core
    other = lax.axis_index("zl") * 2 + 1 - core

    mine = jnp.concatenate([gate_weight[0], up_weight[0]], axis=1)
    mine = with_layout_constraint(mine, Layout(major_to_minor=(0, 1)))
    own_down, mine = lax.optimization_barrier((down_weight[0], mine))
    full_both = lax.all_gather(mine, "x", axis=0, tiled=True)
    from_next = pass_on(own_down, "x", -1)
    from_last = pass_on(own_down, "x", 1)

    turned = roll_columns(cotangent, group * quarter)
    packed = jnp.concatenate([tokens, meta_columns(expert_ids, gate_probs), turned], axis=1)
    wide = width + META
    by_z = lax.all_gather(packed[None], ("zh", "zl"), axis=0, tiled=True)
    by_z, from_next, from_last = lax.optimization_barrier((by_z, from_next, from_last))
    by_z = by_z.reshape(-1, packed.shape[1])
    plane = gather_by_exchange(by_z[:, :wide], "y", y_size)
    cot_z, plane = lax.optimization_barrier((by_z[:, wide:], plane))
    cot_plane = gather_by_exchange(cot_z, "y", y_size)
    if quarters == 4:
        cut = quarter // 2
        across = pass_on(from_next[:, :cut], "x", -1), pass_on(from_last[:, cut:], "x", 1)
        plane, across = lax.optimization_barrier((plane, across))
        downs = [own_down, from_next, *across, from_last]
    else:
        downs = [own_down, from_next]

    count = plane.shape[0]
    code = plane[:, width : width + 2].astype(jnp.int32)
    place = lax.broadcasted_iota(jnp.int32, (count, 1), 0)
    table_own = slot_table(code, place, expert, block)
    table_other = slot_table(code, place, other, block)
    half = table_own.shape[1]

    def arrive(x):
        rows_other = dot(table_other, x, FIRST).astype(BF16)
        arrived = lax.ppermute(rows_other, "c", [(0, 1), (1, 0)])
        return jnp.concatenate([dot(table_own, x, FIRST).astype(BF16), arrived], axis=0)

    rows = arrive(plane)

    def low_first(x):
        split = x.reshape(y_size, high_size, low_size, block, x.shape[1])
        return split.transpose(0, 2, 1, 3, 4).reshape(x.shape)

    code_back = low_first(code)
    place_back = low_first(place)
    back_own = slot_table(code_back, place_back, expert, block)
    back_other = slot_table(code_back, place_back, other, block)

    about = rows[:, width:].astype(F32)
    slot = lax.broadcasted_iota(jnp.int32, (2 * half, 1), 0)
    first = about[:, 0:1].astype(jnp.int32) == expert * CAP + slot % CAP
    prob0 = about[:, 2:3] + about[:, 4:5] + about[:, 6:7]
    prob1 = about[:, 3:4] + about[:, 5:6] + about[:, 7:8]
    prob = jnp.where(first, prob0, prob1)
    token_rows = rows[:, :width]

    def leave(part):
        returned = lax.ppermute(part[half:], "c", [(0, 1), (1, 0)])
        return (dot(back_own, part[:half]) + dot(back_other, returned)).astype(BF16)

    gate_up = dot(token_rows, full_both)
    gate_pre, up_pre = gate_up[:, :ff], gate_up[:, ff:]
    sigmoid_gate = jax.nn.sigmoid(gate_pre)
    activated = gate_pre * sigmoid_gate
    slope_gate = sigmoid_gate * (1.0 + gate_pre * (1.0 - sigmoid_gate))
    hidden = (activated * up_pre).astype(BF16)
    out_part = jnp.concatenate([(prob * dot(hidden, down)).astype(BF16) for down in downs], axis=1)
    out_tokens = leave(out_part)
    out_y = scatter_sum_by_exchange(out_tokens, "y", y_size)

    cot_plane, _ = lax.optimization_barrier((cot_plane, out_tokens))
    cot_rows = (prob * arrive(cot_plane).astype(F32)).astype(BF16)
    grad_hidden = product(cot_rows, downs)
    grad_up = (grad_hidden * activated).astype(BF16)
    grad_gate = (grad_hidden * up_pre * slope_gate).astype(BF16)
    grad_both = jnp.concatenate([grad_gate, grad_up], axis=1)
    grad_tokens = leave(dot(grad_both, full_both, LAST).astype(BF16))
    out_y, grad_tokens = lax.optimization_barrier((out_y, grad_tokens))

    late_hidden, late_cot, _ = lax.optimization_barrier((hidden, cot_rows, grad_tokens))
    partial_down = []
    for q in range(quarters):
        start = lax.rem(q - group + quarters, quarters) * quarter
        block_q = lax.dynamic_slice_in_dim(late_cot, start, quarter, axis=1)
        partial_down.append(dot(late_hidden, block_q, FIRST).astype(BF16))
    down_grads = lax.psum_scatter(jnp.stack(partial_down), "x", scatter_dimension=0)[None]

    grad_y = scatter_sum_by_exchange(grad_tokens, "y", y_size)
    out_low = add_up(send_by_shifts(out_y, "zl", low_size))
    out_low, grad_y = lax.optimization_barrier((out_low, grad_y))
    grad_low = scatter_sum_by_exchange(grad_y, "zl", low_size)
    low = jnp.concatenate([out_low, grad_low], axis=1)
    own = scatter_sum_by_exchange(low, "zh", high_size)
    turn_back = lax.rem(quarters - group, quarters) * quarter
    return roll_columns(own[:, :width], turn_back), own[:, width:], down_grads


def finer(mesh):
    dp, experts, etp = (mesh.shape[name] for name in ("dp", "expert", "etp"))
    high = 4 if etp % 4 == 0 else 2
    shape = (dp, experts // 2, 2, high, etp // high)
    return Mesh(mesh.devices.reshape(shape), ("x", "zl", "c", "zh", "y"))


def solution(mesh):
    rows = P(("x", "zl", "c", "zh", "y"), None)
    columns = P(("zl", "c"), "x", ("zh", "y"))
    depth = P(("zl", "c"), ("zh", "y"), "x")
    return jax.shard_map(
        on_device,
        mesh=finer(mesh),
        in_specs=(rows, rows, rows, columns, columns, depth, rows),
        out_specs=(rows, rows, depth),
        check_vma=False,
    )
```

```python
import jax
import jax.numpy as jnp
from jax import lax
from jax.experimental import pallas as pl
from jax.experimental.layout import Layout, with_layout_constraint
from jax.experimental.pallas import tpu as pltpu
from jax.sharding import Mesh
from jax.sharding import PartitionSpec as P

CAP = 2
META = 128
F32 = jnp.float32
BF16 = jnp.bfloat16
LAST = (((1,), (1,)), ((), ()))
FIRST = (((0,), (0,)), ((), ()))


def dot(a, b, dims=(((1,), (0,)), ((), ()))):
    return lax.dot_general(a, b, dims, preferred_element_type=F32)


def meta_columns(expert_ids, gate_probs):
    rows = expert_ids.shape[0]
    same = expert_ids[:, :, None, None] == expert_ids[None, None, :, :]
    earlier = jnp.arange(rows)[None, None, :, None] < jnp.arange(rows)[:, None, None, None]
    place = jnp.sum((same & earlier).astype(jnp.int32), axis=(2, 3))
    code = (expert_ids * CAP + place).astype(F32)
    high = lax.reduce_precision(gate_probs, 8, 7)
    rest = gate_probs - high
    middle = lax.reduce_precision(rest, 8, 7)
    low = rest - middle
    columns = jnp.concatenate([code, high, middle, low], axis=1).astype(BF16)
    return jnp.pad(columns, ((0, 0), (0, META - columns.shape[1])))


def slot_table(code, token, expert, block):
    slots = code.shape[0] // block * CAP
    slot = lax.broadcasted_iota(jnp.int32, (1, slots), 1)
    wanted = expert * CAP + slot % CAP
    hit = (code[:, 0:1] == wanted) | (code[:, 1:2] == wanted)
    return (hit & (token // block == slot // CAP)).astype(BF16)


def gather_by_exchange(x, axes, size):
    spread = jnp.broadcast_to(x[None], (size,) + x.shape)
    return lax.all_to_all(spread, axes, split_axis=0, concat_axis=0, tiled=True).reshape(
        (size * x.shape[0],) + x.shape[1:]
    )


def scatter_sum_by_exchange(x, axes, size):
    parts = x.reshape((size, x.shape[0] // size) + x.shape[1:])
    parts = lax.all_to_all(parts, axes, split_axis=0, concat_axis=0, tiled=True)
    return jnp.sum(parts.astype(F32), axis=0).astype(BF16)


def send_by_shifts(x, axis, size):
    rows = x.shape[0] // size
    here = lax.axis_index(axis)

    def block(shift):
        return lax.dynamic_slice_in_dim(x, lax.rem(here + shift, size) * rows, rows, axis=0)

    parts = [block(0)]
    for shift in range(1, size):
        pairs = [(i, (i + shift) % size) for i in range(size)]
        parts.append(lax.ppermute(block(shift), axis, pairs))
    return parts


def add_up(parts):
    return sum(part.astype(F32) for part in parts).astype(BF16)


def pass_on(x, axis, shift):
    size = lax.axis_size(axis)
    return lax.ppermute(x, axis, [(i, (i + shift) % size) for i in range(size)])


VMEM = pl.BlockSpec(memory_space=pltpu.VMEM)
PARAMS = pltpu.CompilerParams(vmem_limit_bytes=24 * 1024 * 1024)


def product_kernel(*refs):
    rows_ref, block_refs, total_ref = refs[0], refs[1:-1], refs[-1]
    column, total = 0, 0.0
    for block_ref in block_refs:
        size = block_ref.shape[1]
        piece = rows_ref[:, column : column + size]
        total, column = total + dot(piece, block_ref[...], LAST), column + size
    total_ref[...] = total


def product(rows, blocks):
    return pl.pallas_call(
        product_kernel,
        out_shape=jax.ShapeDtypeStruct((rows.shape[0], blocks[0].shape[0]), F32),
        in_specs=[VMEM] * (1 + len(blocks)),
        out_specs=VMEM,
        compiler_params=PARAMS,
        cost_estimate=pl.CostEstimate(flops=1000, bytes_accessed=1000, transcendentals=0),
    )(rows, *blocks)


def scaled_kernel(hidden_ref, scale_ref, *refs):
    block_refs, first_ref, second_ref = refs[:-2], refs[-2], refs[-1]
    half, column = first_ref.shape[0], 0
    for block_ref in block_refs:
        end = column + block_ref.shape[1]
        result = (scale_ref[...] * dot(hidden_ref[...], block_ref[...])).astype(BF16)
        first_ref[:, column:end] = result[:half]
        second_ref[:, column:end] = result[half:]
        column = end


def scaled_product(hidden, scale, blocks):
    count, depth = hidden.shape
    width = sum(block.shape[1] for block in blocks)
    half = jax.ShapeDtypeStruct((count // 2, width), BF16)
    return pl.pallas_call(
        scaled_kernel,
        out_shape=(half, half),
        in_specs=[VMEM] * (2 + len(blocks)),
        out_specs=(VMEM, VMEM),
        compiler_params=PARAMS,
        cost_estimate=pl.CostEstimate(
            flops=2 * count * depth * width,
            bytes_accessed=2 * (count + depth) * width,
            transcendentals=0,
        ),
    )(hidden, scale, *blocks)


def roll_columns(x, start):
    return lax.dynamic_slice_in_dim(jnp.concatenate([x, x], axis=1), start, x.shape[1], axis=1)


def on_device(tokens, expert_ids, gate_probs, gate_weight, up_weight, down_weight, cotangent):
    block, width = tokens.shape
    ff = gate_weight.shape[2]
    quarter = down_weight.shape[2]
    quarters = width // quarter
    y_size, low_size, high_size = (lax.axis_size(name) for name in ("y", "zl", "zh"))
    group = lax.axis_index("x")
    core = lax.axis_index("c")
    expert = lax.axis_index("zl") * 2 + core
    other = lax.axis_index("zl") * 2 + 1 - core

    mine = jnp.concatenate([gate_weight[0], up_weight[0]], axis=1)
    mine = with_layout_constraint(mine, Layout(major_to_minor=(0, 1)))
    own_down, mine = lax.optimization_barrier((down_weight[0], mine))
    full_both = lax.all_gather(mine, "x", axis=0, tiled=True)
    from_next = pass_on(own_down, "x", -1)
    from_last = pass_on(own_down, "x", 1)

    turned = roll_columns(cotangent, group * quarter)
    packed = jnp.concatenate([tokens, turned, meta_columns(expert_ids, gate_probs)], axis=1)
    by_z = lax.all_gather(packed[None], ("zh", "zl"), axis=0, tiled=True)
    by_z, from_next, from_last = lax.optimization_barrier((by_z, from_next, from_last))
    plane = gather_by_exchange(by_z.reshape(-1, packed.shape[1]), "y", y_size)
    if quarters == 4:
        cut = quarter // 2
        across = pass_on(from_next[:, :cut], "x", -1), pass_on(from_last[:, cut:], "x", 1)
        plane, across = lax.optimization_barrier((plane, across))
        downs = [own_down, from_next, *across, from_last]
    else:
        downs = [own_down, from_next]

    count = plane.shape[0]
    code = plane[:, 2 * width : 2 * width + 2].astype(jnp.int32)
    place = lax.broadcasted_iota(jnp.int32, (count, 1), 0)
    table_own = slot_table(code, place, expert, block)
    table_other = slot_table(code, place, other, block)
    half = table_own.shape[1]
    rows_own = dot(table_own, plane, FIRST).astype(BF16)
    rows_other = dot(table_other, plane, FIRST).astype(BF16)
    rows_arrived = lax.ppermute(rows_other, "c", [(0, 1), (1, 0)])
    rows = jnp.concatenate([rows_own, rows_arrived], axis=0)

    def low_first(x):
        split = x.reshape(y_size, high_size, low_size, block, x.shape[1])
        return split.transpose(0, 2, 1, 3, 4).reshape(x.shape)

    code_back = low_first(code)
    place_back = low_first(place)
    back_own = slot_table(code_back, place_back, expert, block)
    back_other = slot_table(code_back, place_back, other, block)

    about = rows[:, 2 * width :].astype(F32)
    slot = lax.broadcasted_iota(jnp.int32, (2 * half, 1), 0)
    first = about[:, 0:1].astype(jnp.int32) == expert * CAP + slot % CAP
    prob0 = about[:, 2:3] + about[:, 4:5] + about[:, 6:7]
    prob1 = about[:, 3:4] + about[:, 5:6] + about[:, 7:8]
    prob = jnp.where(first, prob0, prob1)
    token_rows = rows[:, :width]

    def leave(here, there):
        returned = lax.ppermute(there, "c", [(0, 1), (1, 0)])
        return (dot(back_own, here) + dot(back_other, returned)).astype(BF16)

    gate_up = dot(token_rows, full_both)
    gate_pre, up_pre = gate_up[:, :ff], gate_up[:, ff:]
    sigmoid_gate = jax.nn.sigmoid(gate_pre)
    activated = gate_pre * sigmoid_gate
    slope_gate = sigmoid_gate * (1.0 + gate_pre * (1.0 - sigmoid_gate))
    hidden = (activated * up_pre).astype(BF16)
    cot_given, hidden = lax.optimization_barrier((rows[:, width : 2 * width], hidden))
    cot_rows = (prob * cot_given.astype(F32)).astype(BF16)
    out_here, out_there = scaled_product(hidden, prob, downs)
    out_tokens = leave(out_here, out_there)
    out_y = scatter_sum_by_exchange(out_tokens, "y", y_size)

    late_cot, _ = lax.optimization_barrier((cot_rows, out_tokens))
    grad_hidden = product(late_cot, downs)
    grad_up = (grad_hidden * activated).astype(BF16)
    grad_gate = (grad_hidden * up_pre * slope_gate).astype(BF16)
    grad_both = jnp.concatenate([grad_gate, grad_up], axis=1)
    late_hidden, _ = lax.optimization_barrier((hidden, out_tokens))
    grad_part = dot(grad_both, full_both, LAST).astype(BF16)
    grad_tokens = leave(grad_part[:half], grad_part[half:])
    partial_down = []
    for q in range(quarters):
        start = lax.rem(q - group + quarters, quarters) * quarter
        block_q = lax.dynamic_slice_in_dim(late_cot, start, quarter, axis=1)
        partial_down.append(dot(late_hidden, block_q, FIRST).astype(BF16))
    partial_down = jnp.stack(partial_down)
    out_y, grad_tokens, partial_down = lax.optimization_barrier((out_y, grad_tokens, partial_down))
    down_grads = lax.psum_scatter(partial_down, "x", scatter_dimension=0)[None]

    grad_y = scatter_sum_by_exchange(grad_tokens, "y", y_size)
    out_low = add_up(send_by_shifts(out_y, "zl", low_size))
    out_low, grad_y = lax.optimization_barrier((out_low, grad_y))
    grad_low = scatter_sum_by_exchange(grad_y, "zl", low_size)
    low = jnp.concatenate([out_low, grad_low], axis=1)
    own = scatter_sum_by_exchange(low, "zh", high_size)
    turn_back = lax.rem(quarters - group, quarters) * quarter
    return roll_columns(own[:, :width], turn_back), own[:, width:], down_grads


def finer(mesh):
    dp, experts, etp = (mesh.shape[name] for name in ("dp", "expert", "etp"))
    high = 4 if etp % 4 == 0 else 2
    shape = (dp, experts // 2, 2, high, etp // high)
    return Mesh(mesh.devices.reshape(shape), ("x", "zl", "c", "zh", "y"))


def solution(mesh):
    rows = P(("x", "zl", "c", "zh", "y"), None)
    columns = P(("zl", "c"), "x", ("zh", "y"))
    depth = P(("zl", "c"), ("zh", "y"), "x")
    return jax.shard_map(
        on_device,
        mesh=finer(mesh),
        in_specs=(rows, rows, rows, columns, columns, depth, rows),
        out_specs=(rows, rows, depth),
        check_vma=False,
    )
```

```python
import jax
import jax.numpy as jnp
from jax import lax
from jax.experimental.layout import Layout, with_layout_constraint
from jax.sharding import Mesh
from jax.sharding import PartitionSpec as P

CAP = 2
META = 128
F32 = jnp.float32
BF16 = jnp.bfloat16
LAST = (((1,), (1,)), ((), ()))
FIRST = (((0,), (0,)), ((), ()))


def dot(a, b, dims=(((1,), (0,)), ((), ()))):
    return lax.dot_general(a, b, dims, preferred_element_type=F32)


def meta_columns(expert_ids, gate_probs):
    rows = expert_ids.shape[0]
    same = expert_ids[:, :, None, None] == expert_ids[None, None, :, :]
    earlier = jnp.arange(rows)[None, None, :, None] < jnp.arange(rows)[:, None, None, None]
    place = jnp.sum((same & earlier).astype(jnp.int32), axis=(2, 3))
    code = (expert_ids * CAP + place).astype(F32)
    high = lax.reduce_precision(gate_probs, 8, 7)
    rest = gate_probs - high
    middle = lax.reduce_precision(rest, 8, 7)
    low = rest - middle
    columns = jnp.concatenate([code, high, middle, low], axis=1).astype(BF16)
    return jnp.pad(columns, ((0, 0), (0, META - columns.shape[1])))


def slot_table(code, token, expert, block):
    slots = code.shape[0] // block * CAP
    slot = lax.broadcasted_iota(jnp.int32, (1, slots), 1)
    wanted = expert * CAP + slot % CAP
    hit = (code[:, 0:1] == wanted) | (code[:, 1:2] == wanted)
    return (hit & (token // block == slot // CAP)).astype(BF16)


def gather_by_exchange(x, axes, size):
    spread = jnp.broadcast_to(x[None], (size,) + x.shape)
    return lax.all_to_all(spread, axes, split_axis=0, concat_axis=0, tiled=True).reshape(
        (size * x.shape[0],) + x.shape[1:]
    )


def scatter_sum_by_exchange(x, axes, size):
    parts = x.reshape((size, x.shape[0] // size) + x.shape[1:])
    parts = lax.all_to_all(parts, axes, split_axis=0, concat_axis=0, tiled=True)
    return jnp.sum(parts.astype(F32), axis=0).astype(BF16)


def send_by_shifts(x, axis, size):
    rows = x.shape[0] // size
    here = lax.axis_index(axis)

    def block(shift):
        return lax.dynamic_slice_in_dim(x, lax.rem(here + shift, size) * rows, rows, axis=0)

    parts = [block(0)]
    for shift in range(1, size):
        pairs = [(i, (i + shift) % size) for i in range(size)]
        parts.append(lax.ppermute(block(shift), axis, pairs))
    return parts


def add_up(parts):
    return sum(part.astype(F32) for part in parts).astype(BF16)


def pass_on(x, axis, shift):
    size = lax.axis_size(axis)
    return lax.ppermute(x, axis, [(i, (i + shift) % size) for i in range(size)])


def roll_columns(x, start):
    return lax.dynamic_slice_in_dim(jnp.concatenate([x, x], axis=1), start, x.shape[1], axis=1)


def on_device(tokens, expert_ids, gate_probs, gate_weight, up_weight, down_weight, cotangent):
    block, width = tokens.shape
    ff = gate_weight.shape[2]
    quarter = down_weight.shape[2]
    quarters = width // quarter
    y_size, low_size, high_size = (lax.axis_size(name) for name in ("y", "zl", "zh"))
    group = lax.axis_index("x")
    core = lax.axis_index("c")
    expert = lax.axis_index("zl") * 2 + core
    other = lax.axis_index("zl") * 2 + 1 - core

    mine = jnp.concatenate([gate_weight[0], up_weight[0]], axis=1)
    mine = with_layout_constraint(mine, Layout(major_to_minor=(0, 1)))
    own_down, mine = lax.optimization_barrier((down_weight[0], mine))
    full_both = lax.all_gather(mine, "x", axis=0, tiled=True)
    from_next = pass_on(own_down, "x", -1)
    from_last = pass_on(own_down, "x", 1)

    turned = roll_columns(cotangent, group * quarter)
    packed = jnp.concatenate([tokens, turned, meta_columns(expert_ids, gate_probs)], axis=1)
    by_z = lax.all_gather(packed[None], ("zh", "zl"), axis=0, tiled=True)
    by_z, from_next, from_last = lax.optimization_barrier((by_z, from_next, from_last))
    plane = gather_by_exchange(by_z.reshape(-1, packed.shape[1]), "y", y_size)
    if quarters == 4:
        cut = quarter // 2
        across = pass_on(from_next[:, :cut], "x", -1), pass_on(from_last[:, cut:], "x", 1)
        full_down = jnp.concatenate([own_down, from_next, *across, from_last], axis=1)
    else:
        full_down = jnp.concatenate([own_down, from_next], axis=1)
    plane, full_down = lax.optimization_barrier((plane, full_down))

    count = plane.shape[0]
    code = plane[:, 2 * width : 2 * width + 2].astype(jnp.int32)
    place = lax.broadcasted_iota(jnp.int32, (count, 1), 0)
    table_own = slot_table(code, place, expert, block)
    table_other = slot_table(code, place, other, block)
    half = table_own.shape[1]
    rows_own = dot(table_own, plane, FIRST).astype(BF16)
    rows_other = dot(table_other, plane, FIRST).astype(BF16)
    rows_arrived = lax.ppermute(rows_other, "c", [(0, 1), (1, 0)])
    rows = jnp.concatenate([rows_own, rows_arrived], axis=0)

    def low_first(x):
        split = x.reshape(y_size, high_size, low_size, block, x.shape[1])
        return split.transpose(0, 2, 1, 3, 4).reshape(x.shape)

    code_back = low_first(code)
    place_back = low_first(place)
    back = [slot_table(code_back, place_back, which, block) for which in (expert, other)]
    back = lax.optimization_barrier(jnp.concatenate(back, axis=1))

    about = rows[:, 2 * width :].astype(F32)
    slot = lax.broadcasted_iota(jnp.int32, (2 * half, 1), 0)
    first = about[:, 0:1].astype(jnp.int32) == expert * CAP + slot % CAP
    prob0 = about[:, 2:3] + about[:, 4:5] + about[:, 6:7]
    prob1 = about[:, 3:4] + about[:, 5:6] + about[:, 7:8]
    prob = jnp.where(first, prob0, prob1)
    token_rows = rows[:, :width]

    def swap_back(part):
        return jnp.concatenate([part[:half], lax.ppermute(part[half:], "c", [(0, 1), (1, 0)])])

    def by_token(rows_back):
        return dot(back, rows_back).astype(BF16)

    gate_up = dot(token_rows, full_both)
    gate_pre, up_pre = gate_up[:, :ff], gate_up[:, ff:]
    sigmoid_gate = jax.nn.sigmoid(gate_pre)
    activated = gate_pre * sigmoid_gate
    slope_gate = sigmoid_gate * (1.0 + gate_pre * (1.0 - sigmoid_gate))
    hidden = (activated * up_pre).astype(BF16)
    late_prob, hidden = lax.optimization_barrier((prob, hidden))
    cot_rows = (late_prob * rows[:, width : 2 * width].astype(F32)).astype(BF16)
    out_part = (prob * dot(hidden, full_down)).astype(BF16)
    out_tokens = by_token(swap_back(out_part))
    out_y = scatter_sum_by_exchange(out_tokens, "y", y_size)

    late_cot, _ = lax.optimization_barrier((cot_rows, out_tokens))
    grad_hidden = dot(late_cot, full_down, LAST)
    grad_up = (grad_hidden * activated).astype(BF16)
    grad_gate = (grad_hidden * up_pre * slope_gate).astype(BF16)
    grad_both = jnp.concatenate([grad_gate, grad_up], axis=1)
    late_hidden, _ = lax.optimization_barrier((hidden, out_part))
    grad_both, _ = lax.optimization_barrier((grad_both, out_tokens))
    grad_part = dot(grad_both, full_both, LAST).astype(BF16)
    grad_tokens = by_token(swap_back(grad_part))
    out_y, grad_tokens = lax.optimization_barrier((out_y, grad_tokens))
    partial_down = []
    for q in range(quarters):
        start = lax.rem(q - group + quarters, quarters) * quarter
        block_q = lax.dynamic_slice_in_dim(cot_rows, start, quarter, axis=1)
        partial_down.append(dot(late_hidden, block_q, FIRST).astype(BF16))
    partial_down = jnp.stack(partial_down)
    down_grads = lax.psum_scatter(partial_down, "x", scatter_dimension=0)[None]

    grad_y = scatter_sum_by_exchange(grad_tokens, "y", y_size)
    out_low = add_up(send_by_shifts(out_y, "zl", low_size))
    out_low, grad_y = lax.optimization_barrier((out_low, grad_y))
    grad_low = scatter_sum_by_exchange(grad_y, "zl", low_size)
    low = jnp.concatenate([out_low, grad_low], axis=1)
    own = scatter_sum_by_exchange(low, "zh", high_size)
    turn_back = lax.rem(quarters - group, quarters) * quarter
    return roll_columns(own[:, :width], turn_back), own[:, width:], down_grads


def finer(mesh):
    dp, experts, etp = (mesh.shape[name] for name in ("dp", "expert", "etp"))
    high = 4 if etp % 4 == 0 else 2
    shape = (dp, experts // 2, 2, high, etp // high)
    return Mesh(mesh.devices.reshape(shape), ("x", "zl", "c", "zh", "y"))


def solution(mesh):
    rows = P(("x", "zl", "c", "zh", "y"), None)
    columns = P(("zl", "c"), "x", ("zh", "y"))
    depth = P(("zl", "c"), ("zh", "y"), "x")
    return jax.shard_map(
        on_device,
        mesh=finer(mesh),
        in_specs=(rows, rows, rows, columns, columns, depth, rows),
        out_specs=(rows, rows, depth),
        check_vma=False,
    )
```

```python
import jax
import jax.numpy as jnp
from jax import lax
from jax.experimental.layout import Layout, with_layout_constraint
from jax.sharding import Mesh
from jax.sharding import PartitionSpec as P

CAP = 2
META = 128
F32 = jnp.float32
BF16 = jnp.bfloat16
LAST = (((1,), (1,)), ((), ()))
FIRST = (((0,), (0,)), ((), ()))


def dot(a, b, dims=(((1,), (0,)), ((), ()))):
    return lax.dot_general(a, b, dims, preferred_element_type=F32)


def meta_columns(expert_ids, gate_probs):
    rows = expert_ids.shape[0]
    same = expert_ids[:, :, None, None] == expert_ids[None, None, :, :]
    earlier = jnp.arange(rows)[None, None, :, None] < jnp.arange(rows)[:, None, None, None]
    place = jnp.sum((same & earlier).astype(jnp.int32), axis=(2, 3))
    code = (expert_ids * CAP + place).astype(F32)
    high = lax.reduce_precision(gate_probs, 8, 7)
    rest = gate_probs - high
    middle = lax.reduce_precision(rest, 8, 7)
    low = rest - middle
    columns = jnp.concatenate([code, high, middle, low], axis=1).astype(BF16)
    return jnp.pad(columns, ((0, 0), (0, META - columns.shape[1])))


def slot_table(code, token, expert, block):
    slots = code.shape[0] // block * CAP
    slot = lax.broadcasted_iota(jnp.int32, (1, slots), 1)
    wanted = expert * CAP + slot % CAP
    hit = (code[:, 0:1] == wanted) | (code[:, 1:2] == wanted)
    return (hit & (token // block == slot // CAP)).astype(BF16)


def gather_by_exchange(x, axes, size):
    spread = jnp.broadcast_to(x[None], (size,) + x.shape)
    return lax.all_to_all(spread, axes, split_axis=0, concat_axis=0, tiled=True).reshape(
        (size * x.shape[0],) + x.shape[1:]
    )


def scatter_sum_by_exchange(x, axes, size):
    parts = x.reshape((size, x.shape[0] // size) + x.shape[1:])
    parts = lax.all_to_all(parts, axes, split_axis=0, concat_axis=0, tiled=True)
    return jnp.sum(parts.astype(F32), axis=0).astype(BF16)


def send_by_shifts(x, axis, size):
    rows = x.shape[0] // size
    here = lax.axis_index(axis)

    def block(shift):
        return lax.dynamic_slice_in_dim(x, lax.rem(here + shift, size) * rows, rows, axis=0)

    parts = [block(0)]
    for shift in range(1, size):
        pairs = [(i, (i + shift) % size) for i in range(size)]
        parts.append(lax.ppermute(block(shift), axis, pairs))
    return parts


def add_up(parts):
    return sum(part.astype(F32) for part in parts).astype(BF16)


def pass_on(x, axis, shift):
    size = lax.axis_size(axis)
    return lax.ppermute(x, axis, [(i, (i + shift) % size) for i in range(size)])


def roll_columns(x, start):
    return lax.dynamic_slice_in_dim(jnp.concatenate([x, x], axis=1), start, x.shape[1], axis=1)


def on_device(tokens, expert_ids, gate_probs, gate_weight, up_weight, down_weight, cotangent):
    block, width = tokens.shape
    ff = gate_weight.shape[2]
    quarter = down_weight.shape[2]
    quarters = width // quarter
    y_size, low_size, high_size = (lax.axis_size(name) for name in ("y", "zl", "zh"))
    group = lax.axis_index("x")
    core = lax.axis_index("c")
    expert = lax.axis_index("zl") * 2 + core
    other = lax.axis_index("zl") * 2 + 1 - core

    mine = jnp.concatenate([gate_weight[0], up_weight[0]], axis=1)
    mine = with_layout_constraint(mine, Layout(major_to_minor=(0, 1)))
    own_down, mine = lax.optimization_barrier((down_weight[0], mine))
    full_both = lax.all_gather(mine, "x", axis=0, tiled=True)
    from_next = pass_on(own_down, "x", -1)
    from_last = pass_on(own_down, "x", 1)

    turned = roll_columns(cotangent, group * quarter)
    packed = jnp.concatenate([tokens, turned, meta_columns(expert_ids, gate_probs)], axis=1)
    by_z = lax.all_gather(packed[None], ("zh", "zl"), axis=0, tiled=True)
    by_z, from_next, from_last = lax.optimization_barrier((by_z, from_next, from_last))
    plane = gather_by_exchange(by_z.reshape(-1, packed.shape[1]), "y", y_size)
    if quarters == 4:
        cut = quarter // 2
        across = pass_on(from_next[:, :cut], "x", -1), pass_on(from_last[:, cut:], "x", 1)
        full_down = jnp.concatenate([own_down, from_next, *across, from_last], axis=1)
    else:
        full_down = jnp.concatenate([own_down, from_next], axis=1)
    plane, full_down = lax.optimization_barrier((plane, full_down))

    count = plane.shape[0]
    code = plane[:, 2 * width : 2 * width + 2].astype(jnp.int32)
    place = lax.broadcasted_iota(jnp.int32, (count, 1), 0)
    table_own = slot_table(code, place, expert, block)
    table_other = slot_table(code, place, other, block)
    half = table_own.shape[1]
    rows_own = dot(table_own, plane, FIRST).astype(BF16)
    rows_other = dot(table_other, plane, FIRST).astype(BF16)
    rows_arrived = lax.ppermute(rows_other, "c", [(0, 1), (1, 0)])
    rows = jnp.concatenate([rows_own, rows_arrived], axis=0)

    def low_first(x):
        split = x.reshape(y_size, high_size, low_size, block, x.shape[1])
        return split.transpose(0, 2, 1, 3, 4).reshape(x.shape)

    code_back = low_first(code)
    place_back = low_first(place)
    back = [slot_table(code_back, place_back, which, block) for which in (expert, other)]
    back = lax.optimization_barrier(jnp.concatenate(back, axis=1))

    about = rows[:, 2 * width :].astype(F32)
    slot = lax.broadcasted_iota(jnp.int32, (2 * half, 1), 0)
    first = about[:, 0:1].astype(jnp.int32) == expert * CAP + slot % CAP
    prob0 = about[:, 2:3] + about[:, 4:5] + about[:, 6:7]
    prob1 = about[:, 3:4] + about[:, 5:6] + about[:, 7:8]
    prob = jnp.where(first, prob0, prob1)
    token_rows = rows[:, :width]

    def swap_back(part):
        return jnp.concatenate([part[:half], lax.ppermute(part[half:], "c", [(0, 1), (1, 0)])])

    def by_token(rows_back):
        return dot(back, rows_back).astype(BF16)

    gate_up = dot(token_rows, full_both)
    gate_pre, up_pre = gate_up[:, :ff], gate_up[:, ff:]
    sigmoid_gate = jax.nn.sigmoid(gate_pre)
    activated = gate_pre * sigmoid_gate
    slope_gate = sigmoid_gate * (1.0 + gate_pre * (1.0 - sigmoid_gate))
    hidden = (activated * up_pre).astype(BF16)
    late_prob, hidden = lax.optimization_barrier((prob, hidden))
    cot_rows = (late_prob * rows[:, width : 2 * width].astype(F32)).astype(BF16)
    out_part = (prob * dot(hidden, full_down)).astype(BF16)
    out_tokens = by_token(swap_back(out_part))
    out_y = scatter_sum_by_exchange(out_tokens, "y", y_size)

    late_cot, _ = lax.optimization_barrier((cot_rows, out_tokens))
    grad_hidden = dot(late_cot, full_down, LAST)
    grad_up = (grad_hidden * activated).astype(BF16)
    grad_gate = (grad_hidden * up_pre * slope_gate).astype(BF16)
    grad_both = jnp.concatenate([grad_gate, grad_up], axis=1)
    late_hidden, _ = lax.optimization_barrier((hidden, out_tokens))
    grad_both, _ = lax.optimization_barrier((grad_both, out_tokens))
    grad_part = dot(grad_both, full_both, LAST).astype(BF16)
    grad_tokens = by_token(swap_back(grad_part))
    out_y, grad_tokens = lax.optimization_barrier((out_y, grad_tokens))
    partial_down = []
    for q in range(quarters):
        start = lax.rem(q - group + quarters, quarters) * quarter
        block_q = lax.dynamic_slice_in_dim(cot_rows, start, quarter, axis=1)
        partial_down.append(dot(late_hidden, block_q, FIRST).astype(BF16))
    partial_down = jnp.stack(partial_down)
    down_grads = lax.psum_scatter(partial_down, "x", scatter_dimension=0)[None]

    grad_y = scatter_sum_by_exchange(grad_tokens, "y", y_size)
    out_low = add_up(send_by_shifts(out_y, "zl", low_size))
    out_low, grad_y = lax.optimization_barrier((out_low, grad_y))
    grad_low = scatter_sum_by_exchange(grad_y, "zl", low_size)
    low = jnp.concatenate([out_low, grad_low], axis=1)
    own = scatter_sum_by_exchange(low, "zh", high_size)
    turn_back = lax.rem(quarters - group, quarters) * quarter
    return roll_columns(own[:, :width], turn_back), own[:, width:], down_grads


def finer(mesh):
    dp, experts, etp = (mesh.shape[name] for name in ("dp", "expert", "etp"))
    high = 4 if etp % 4 == 0 else 2
    shape = (dp, experts // 2, 2, high, etp // high)
    return Mesh(mesh.devices.reshape(shape), ("x", "zl", "c", "zh", "y"))


def solution(mesh):
    rows = P(("x", "zl", "c", "zh", "y"), None)
    columns = P(("zl", "c"), "x", ("zh", "y"))
    depth = P(("zl", "c"), ("zh", "y"), "x")
    return jax.shard_map(
        on_device,
        mesh=finer(mesh),
        in_specs=(rows, rows, rows, columns, columns, depth, rows),
        out_specs=(rows, rows, depth),
        check_vma=False,
    )
```
